32 devices in a mesh: replica: 2 (over y), tensor: 16 (over z, x, core).
Axes of the slice: x: 2, y: 2, z: 4, core: 2. Of those that a mesh axis runs over, the one named last changes fastest.
Arguments:
- activations: bfloat16 [8192, 832], P(('replica', 'tensor')), may hold values from -6 to 6
- out_grad: bfloat16 [8192, 7168], P('replica', 'tensor'), may hold values from -0.09375 to 0.09375
- master_weights: float32 [1664, 7168], P('replica', 'tensor'), may hold values from -6 to 6
- first_moment: float32 [1664, 7168], P('replica', 'tensor'), may hold values from -0.6 to 0.6
- second_moment: float32 [1664, 7168], P('replica', 'tensor'), may hold values from 0.01 to 1
- anchor: float32 [832, 7168], P(None, 'tensor'), may hold values from -6 to 6
- outer_momentum: float32 [832, 7168], P(None, 'tensor'), may hold values from -3 to 3
Outputs:
- rebuilt_weights: bfloat16 [832, 7168], P(None, 'tensor')
- new_momentum: float32 [832, 7168], P(None, 'tensor')
The draws below stay inside these ranges and needn't reach their ends.
All inputs are finite; a program needn't handle non-finite values.
Results may differ from the reference program's by a relative error of at most 0.001.
Values may be sent and summed in bfloat16 or wider, within the bound.
No kernel may reach another device: no remote copies, remote signals or barrier semaphores. Data moves between devices by JAX's collectives and lax.ppermute only.
A program may use at most 128 MiB of HBM per device.

```python
import math
import jax
import jax.numpy as jnp
from jax import lax

FRAG = 832
TOK_DEV = 256
FF = 7168
GROUP_TOK = 4096
ALL_TOK = 8192
ALL_ROWS = 1664
N_REPLICA = 2
N_TENSOR = 16


def steps_of(rng, dims, shards, least, largest):
    loudness = 1.0
    for axis_at, parts in shards:
        steps = jax.random.uniform(jax.random.fold_in(jax.random.fold_in(rng, 6), axis_at), (parts,), jnp.float32, least / len(shards), largest / len(shards))
        loudness = loudness * jnp.repeat(jnp.exp(steps), dims[axis_at] // parts).reshape((-1,) + (1,) * (len(dims) - 1 - axis_at))
    return loudness


def normal_values(stream_key, shape, width, limit, cuts=(), kind=jnp.bfloat16):
    values = width * jax.random.normal(stream_key, shape, jnp.float32)
    if cuts:
        values = values * steps_of(stream_key, shape, cuts, -0.22, 0.18)
    return jnp.clip(values, -limit, limit).astype(kind)


def setup_inputs(seed: int = 0) -> dict:
    arg_keys = jax.random.split(jax.random.key(seed), 8)
    activations = normal_values(arg_keys[0], (ALL_TOK, FRAG), 1.0, 6.0, ((0, 32),))
    out_grad = normal_values(arg_keys[1], (ALL_TOK, FF), GROUP_TOK ** -0.5, 0.09375, ((0, 2), (1, 16)))
    master_weights = normal_values(arg_keys[2], (ALL_ROWS, FF), 1.0, 6.0, ((0, 2), (1, 16)), jnp.float32)
    first_moment = normal_values(arg_keys[3], (ALL_ROWS, FF), 0.1, 0.6, ((0, 2), (1, 16)), jnp.float32)
    second_moment = jnp.clip(jnp.exp(math.log(1.0) - 4.6051702 * jax.random.uniform(arg_keys[4], (ALL_ROWS, FF), jnp.float32) ** steps_of(arg_keys[4], (ALL_ROWS, FF), ((0, 2), (1, 16)), -0.2, 0.2)), 0.01, 1.0)
    anchor = normal_values(arg_keys[5], (FRAG, FF), 1.0, 6.0, ((1, 16),), jnp.float32)
    outer_momentum = normal_values(arg_keys[6], (FRAG, FF), 0.5, 3.0, ((1, 16),), jnp.float32)
    return dict(activations=activations, out_grad=out_grad, master_weights=master_weights, first_moment=first_moment, second_moment=second_moment, anchor=anchor, outer_momentum=outer_momentum)


BETA_ONE = 0.9
BETA_TWO = 0.95
BIAS_ONE = 0.9999734386
BIAS_TWO = 0.9940794708
EPSILON = 1e-08
INNER_RATE = 0.25
DECAY_RATE = 0.1
OUTER_RATE = 0.7
NESTEROV = 0.9

def reference(activations, out_grad, master_weights, first_moment, second_moment, anchor, outer_momentum):
    group_rows = TOK_DEV * N_TENSOR
    summed = jnp.zeros(anchor.shape, jnp.float32)
    for replica_id in range(N_REPLICA):
        block_acts = activations[replica_id * group_rows:(replica_id + 1) * group_rows]
        block_grad = out_grad[replica_id * group_rows:(replica_id + 1) * group_rows]
        gradient = lax.dot_general(block_acts, block_grad, (((0,), (0,)), ((), ())), preferred_element_type=jnp.float32)
        lower = replica_id * FRAG
        weights = master_weights[lower:lower + FRAG]
        moment_one = BETA_ONE * first_moment[lower:lower + FRAG] + (1.0 - BETA_ONE) * gradient
        moment_two = BETA_TWO * second_moment[lower:lower + FRAG] + (1.0 - BETA_TWO) * gradient * gradient
        step_size = moment_one / BIAS_ONE / (jnp.sqrt(moment_two / BIAS_TWO) + EPSILON)
        updated = weights - INNER_RATE * (step_size + DECAY_RATE * weights)
        summed = summed + (anchor - updated)
    pseudo_mean = summed / N_REPLICA
    new_momentum = NESTEROV * outer_momentum + pseudo_mean
    rebuilt = anchor - OUTER_RATE * (pseudo_mean + NESTEROV * new_momentum)
    return (rebuilt.astype(jnp.bfloat16), new_momentum)
```

```python
import functools

import jax
import jax.numpy as jnp
import numpy as np
from jax import lax
from jax.experimental import pallas as pl
from jax.experimental.pallas import tpu as pltpu
from jax.sharding import PartitionSpec as P

BETA_ONE = 0.9
BETA_TWO = 0.95
BIAS_ONE = 0.9999734386
BIAS_TWO = 0.9940794708
EPSILON = 1e-08
INNER_RATE = 0.25
DECAY_RATE = 0.1
OUTER_RATE = 0.7
NESTEROV = 0.9
CORES = 2
LANES = 128


def chip_ring(chips):
    return list(range(0, chips, 2)) + list(range(chips - 1, 0, -2))


def neighbour_exchange(size):
    ring = chip_ring(size // CORES)
    chips = len(ring)
    partner = [[0] * size for _ in range(2)]
    for kind in range(2):
        for core in range(CORES):
            for at in range(chips):
                other = at + 1 if (at + kind + core) % 2 == 0 else at - 1
                partner[kind][ring[at] * CORES + core] = ring[other % chips] * CORES + core
    held = [[d] for d in range(size)]
    sent = [[d] for d in range(size)]
    for step in range(chips // 2):
        came = [sent[partner[step % 2][d]] for d in range(size)]
        held = [h + c for h, c in zip(held, came)]
        sent = [h[:2] for h in held] if step == 0 else came
    pairs = [[(d, p) for d, p in enumerate(kind)] for kind in partner]
    return pairs, np.array(held, np.int32)


def feature_cuts(features):
    tiles = features // LANES
    return [0, LANES * ((tiles + 1) // 2), LANES * (tiles - 1), features]


def gradient_kernel(low, tokens, starts_ref, mine_ref, theirs_ref, own_ref, first_ref, *refs):
    later, (keep_ref, give_ref, grad, acts, sems) = refs[:-5], refs[-5:]
    count = keep_ref.shape[1]
    columns = keep_ref.shape[0]
    blocks = starts_ref.shape[1]
    halves = [[], []]

    def begin(half, source, target):
        copy = pltpu.make_async_copy(source, target, sems.at[sum(map(len, halves))])
        copy.start()
        halves[half].append(copy)

    for at in range(blocks):
        half = at * 2 // blocks
        here = pl.ds(at * tokens, tokens)
        there = pl.ds(pl.multiple_of(starts_ref[0, at] * tokens, LANES), tokens)
        begin(half, mine_ref.at[:, there], grad.at[pl.ds(0, columns), here])
        begin(half, theirs_ref.at[:, there], grad.at[pl.ds(columns, columns), here])
        if at < 2:
            begin(half, (own_ref, first_ref)[at].at[pl.ds(low, count), :], acts.at[:, here])
        elif at % 2 == 0:
            begin(half, later[at // 2 - 1], acts.at[:, pl.ds(at * tokens, 2 * tokens)])
    cut = (blocks // 2) * tokens
    for half, span in enumerate((slice(0, cut), slice(cut, blocks * tokens))):
        for copy in halves[half]:
            copy.wait()
        for at, out in enumerate((keep_ref, give_ref)):
            product = lax.dot_general(
                grad[at * columns : (at + 1) * columns, span],
                acts[:, span],
                (((1,), (1,)), ((), ())),
                preferred_element_type=jnp.float32,
            )
            out[...] = product if half == 0 else out[...] + product


def partial_gradient(low, high, starts, mine, theirs, own, first, later):
    tokens, columns, blocks = own.shape[1], mine.shape[0], starts.shape[1]
    count = high - low
    out = jax.ShapeDtypeStruct((columns, count), jnp.float32)
    return pl.pallas_call(
        functools.partial(gradient_kernel, low, tokens),
        out_shape=(out, out),
        in_specs=[pl.BlockSpec(memory_space=pltpu.SMEM)]
        + [pl.BlockSpec(memory_space=pl.ANY)] * (4 + len(later)),
        out_specs=(pl.BlockSpec(memory_space=pltpu.VMEM),) * 2,
        scratch_shapes=[
            pltpu.VMEM((CORES * columns, blocks * tokens), mine.dtype),
            pltpu.VMEM((count, blocks * tokens), own.dtype),
            pltpu.SemaphoreType.DMA((3 * blocks,)),
        ],
        compiler_params=pltpu.CompilerParams(vmem_limit_bytes=32 * 2**20),
        cost_estimate=pl.CostEstimate(
            flops=2 * CORES * columns * count * blocks * tokens,
            bytes_accessed=2 * (CORES * columns + count) * blocks * tokens + 8 * columns * count,
            transcendentals=0,
        ),
        name="gradient",
    )(starts, mine, theirs, own, first, *later)


def start_to_half(anchor, weights):
    exact = anchor - (1.0 - INNER_RATE * DECAY_RATE) * weights
    return exact, lax.reduce_precision(exact, 5, 10)


def late_part(gradient, first_moment, second_moment, weights, anchor):
    moment_one = BETA_ONE * first_moment + (1.0 - BETA_ONE) * gradient
    moment_two = BETA_TWO * second_moment + (1.0 - BETA_TWO) * gradient * gradient
    step = moment_one / BIAS_ONE / (jnp.sqrt(moment_two / BIAS_TWO) + EPSILON)
    exact, half = start_to_half(anchor, weights)
    return ((exact - half) + INNER_RATE * step).astype(jnp.float16)


def on_device(
    activations, out_grad, master_weights, first_moment, second_moment, anchor, outer_momentum
):
    size = lax.axis_size("tensor")
    groups = lax.axis_size("replica")
    pairs, held = neighbour_exchange(size)
    swap = [(d, d ^ 1) for d in range(size)]
    own, mine = activations.T, out_grad.T
    weights, one, two = master_weights.T, first_moment.T, second_moment.T
    anchor, momentum = anchor.T, outer_momentum.T
    cuts = feature_cuts(own.shape[0])
    spans = list(zip(cuts[:-1], cuts[1:]))
    starts = lax.dynamic_slice_in_dim(jnp.asarray(held), lax.axis_index("tensor"), 1, 0)

    def other_groups_sum(value):
        total = None
        for hop in range(1, groups):
            there = [(g, (g + hop) % groups) for g in range(groups)]
            came = lax.ppermute(value, "replica", there).astype(jnp.float32)
            total = came if total is None else total + came
        return total

    first = lax.ppermute(own, "tensor", pairs[0])
    theirs = lax.ppermute(mine, "tensor", swap)
    early = start_to_half(anchor, weights)[1]
    early_others = other_groups_sum(early.astype(jnp.float16))

    rebuilt = jnp.zeros(anchor.shape, jnp.bfloat16)
    new_momentum = jnp.zeros(anchor.shape, jnp.float32)
    for low, high in spans:
        block = jnp.concatenate([own[low:high], first[low:high]], axis=1)
        later = []
        for step in range(1, held.shape[1] // 2):
            block = lax.ppermute(block, "tensor", pairs[step % 2])
            later.append(block)
        keep, give = partial_gradient(low, high, starts, mine, theirs, own, first, later)
        gradient = keep + lax.ppermute(give, "tensor", swap)
        here = lambda x: x[:, low:high]
        late = late_part(gradient, here(one), here(two), here(weights), here(anchor))
        late_others = other_groups_sum(late)
        mean = ((here(early) + here(early_others)) + (late.astype(jnp.float32) + late_others)) / groups
        moved = NESTEROV * here(momentum) + mean
        weight = here(anchor) - OUTER_RATE * (mean + NESTEROV * moved)
        rebuilt = lax.dynamic_update_slice(rebuilt, weight.astype(jnp.bfloat16), (0, low))
        new_momentum = lax.dynamic_update_slice(new_momentum, moved, (0, low))
    return rebuilt.T, new_momentum.T


def solution(mesh):
    placed = (
        P(("replica", "tensor"), None),
        P("replica", "tensor"),
        P("replica", "tensor"),
        P("replica", "tensor"),
        P("replica", "tensor"),
        P(None, "tensor"),
        P(None, "tensor"),
    )
    return jax.shard_map(
        on_device,
        mesh=mesh,
        in_specs=placed,
        out_specs=(P(None, "tensor"), P(None, "tensor")),
        check_vma=False,
    )
```

```python
import functools

import jax
import jax.numpy as jnp
from jax import lax
from jax.experimental import pallas as pl
from jax.experimental.pallas import tpu as pltpu
from jax.sharding import PartitionSpec as P

BETA_ONE = 0.9
BETA_TWO = 0.95
BIAS_ONE = 0.9999734386
BIAS_TWO = 0.9940794708
EPSILON = 1e-08
INNER_RATE = 0.25
DECAY_RATE = 0.1
OUTER_RATE = 0.7
NESTEROV = 0.9
CORES = 2
LANES = 128


def chip_ring(chips):
    return list(range(0, chips, 2)) + list(range(chips - 1, 0, -2))


def arrivals(chips):
    return [[0]] + [[-hop, hop] for hop in range(1, chips // 2)] + [[chips // 2]]


def ring_step(size, hop):
    ring = chip_ring(size // CORES)
    return [
        (chip * CORES + core, ring[(at + hop) % len(ring)] * CORES + core)
        for at, chip in enumerate(ring)
        for core in range(CORES)
    ]


def feature_cuts(features):
    tiles = features // LANES
    return [0, tiles // 3 * LANES, 2 * (tiles // 3) * LANES, features]

def in_vmem(limit):
    return pltpu.CompilerParams(vmem_limit_bytes=limit)


def sort_kernel(chips, grad_ref, sorted_ref, sems):
    index = lax.axis_index("tensor")
    at, core = index // CORES, index % CORES
    tokens = sorted_ref.shape[1] // (CORES * chips)
    ring = chip_ring(chips)
    place = sum(jnp.where(at == chip, spot, 0) for spot, chip in enumerate(ring))
    copies = []
    for hops in arrivals(chips):
        for side in range(CORES):
            for hop in hops:
                there = lax.rem(place + hop + chips, chips)
                chip = sum(jnp.where(there == s, c, 0) for s, c in enumerate(ring))
                block = chip * CORES + (core if side == 0 else 1 - core)
                copy = pltpu.make_async_copy(
                    grad_ref.at[:, pl.ds(pl.multiple_of(block * tokens, LANES), tokens)],
                    sorted_ref.at[:, pl.ds(len(copies) * tokens, tokens)],
                    sems.at[len(copies)],
                )
                copy.start()
                copies.append(copy)
    for copy in copies:
        copy.wait()


def sort_tokens(grad, chips):
    return pl.pallas_call(
        functools.partial(sort_kernel, chips),
        out_shape=pltpu.VMEM(grad.shape, grad.dtype),
        in_specs=[pl.BlockSpec(memory_space=pl.ANY)],
        out_specs=pl.BlockSpec(memory_space=pltpu.VMEM),
        scratch_shapes=[pltpu.SemaphoreType.DMA((CORES * chips,))],
        compiler_params=in_vmem(2**20),
        cost_estimate=pl.CostEstimate(flops=0, bytes_accessed=4 * grad.size, transcendentals=0),
        name="sort_tokens",
    )(grad)


def place_kernel(low, *refs):
    parts, outs, sems = refs[:2], refs[-3:-1], refs[-1]
    copies = [
        pltpu.make_async_copy(part, out.at[:, pl.ds(low, part.shape[1])], sems.at[at])
        for at, (part, out) in enumerate(zip(parts, outs))
    ]
    for copy in copies:
        copy.start()
    for copy in copies:
        copy.wait()


def place(low, width, parts, outs):
    return pl.pallas_call(
        functools.partial(place_kernel, low),
        out_shape=tuple(jax.ShapeDtypeStruct((p.shape[0], width), p.dtype) for p in parts),
        in_specs=[pl.BlockSpec(memory_space=pl.ANY)] * (2 + len(outs)),
        out_specs=(pl.BlockSpec(memory_space=pl.ANY),) * 2,
        scratch_shapes=[pltpu.SemaphoreType.DMA((2,))],
        input_output_aliases={2 + at: at for at in range(len(outs))},
        compiler_params=in_vmem(2**20),
        cost_estimate=pl.CostEstimate(
            flops=0, bytes_accessed=12 * parts[0].size, transcendentals=0
        ),
        name="place",
    )(*parts, *outs)


def gradient_kernel(low, skip, tops, grad_ref, *refs):
    count = len(tops)
    blocks, so_far, (out_ref, acts, sems) = refs[:count], refs[count:-3], refs[-3:]
    tokens, high = blocks[0].shape[1], low + out_ref.shape[1]
    at, copies = 0, []
    for block, (top, ends) in zip(blocks, tops):
        first, after = max(low, top), min(high, top + block.shape[0])
        if first < after:
            copy = pltpu.make_async_copy(
                block.at[pl.ds(first - top, after - first)],
                acts.at[pl.ds(first - low, after - first), pl.ds(at * tokens, tokens)],
                sems.at[len(copies)],
            )
            copy.start()
            copies.append(copy)
        at += ends
    for copy in copies:
        copy.wait()
    product = lax.dot_general(
        grad_ref[:, skip * tokens : (skip + at) * tokens],
        acts[...],
        (((1,), (1,)), ((), ())),
        preferred_element_type=jnp.float32,
    )
    for ref in so_far:
        product = ref[:, low:high] + product
    out_ref[...] = product


def gradient_part(low, high, skip, grad, blocks, so_far=()):
    rows, tokens = grad.shape[0], blocks[0][0].shape[1]
    arrays = [b[0] for b in blocks]
    depth = tokens * sum(b[2] for b in blocks)
    return pl.pallas_call(
        functools.partial(gradient_kernel, low, skip, [b[1:] for b in blocks]),
        out_shape=jax.ShapeDtypeStruct((rows, high - low), jnp.float32),
        in_specs=[pl.BlockSpec(memory_space=pltpu.VMEM)]
        + [pl.BlockSpec(memory_space=pl.ANY)] * len(arrays)
        + [pl.BlockSpec(memory_space=pltpu.VMEM)] * len(so_far),
        out_specs=pl.BlockSpec(memory_space=pltpu.VMEM),
        scratch_shapes=[
            pltpu.VMEM((high - low, depth), arrays[0].dtype),
            pltpu.SemaphoreType.DMA((len(arrays),)),
        ],
        compiler_params=in_vmem(16 * 2**20),
        cost_estimate=pl.CostEstimate(
            flops=2 * rows * (high - low) * depth, bytes_accessed=8 * rows * (high - low), transcendentals=0
        ),
        name="gradient",
    )(grad, *arrays, *so_far)


def start_to_half(anchor, weights):
    exact = anchor - (1.0 - INNER_RATE * DECAY_RATE) * weights
    return exact, lax.reduce_precision(exact, 5, 10)


def late_part(gradient, first_moment, second_moment, weights, anchor):
    moment_one = BETA_ONE * first_moment + (1.0 - BETA_ONE) * gradient
    moment_two = BETA_TWO * second_moment + (1.0 - BETA_TWO) * gradient * gradient
    step = moment_one / BIAS_ONE / (jnp.sqrt(moment_two / BIAS_TWO) + EPSILON)
    exact, half = start_to_half(anchor, weights)
    return ((exact - half) + INNER_RATE * step).astype(jnp.float16)


def on_device(
    activations, out_grad, master_weights, first_moment, second_moment, anchor, outer_momentum
):
    size = lax.axis_size("tensor")
    groups = lax.axis_size("replica")
    chips = size // CORES
    half = chips // 2
    pairs = {hop: ring_step(size, hop) for hop in (1, -1)}
    swap = [(d, d ^ 1) for d in range(size)]
    own, mine = activations.T, out_grad.T
    weights, one, two = master_weights.T, first_moment.T, second_moment.T
    anchor, momentum = anchor.T, outer_momentum.T
    cuts = feature_cuts(own.shape[0])
    spans = list(zip(cuts[:-1], cuts[1:]))

    def other_groups_sum(value):
        total = None
        for hop in range(1, groups):
            there = [(g, (g + hop) % groups) for g in range(groups)]
            came = lax.ppermute(value, "replica", there).astype(jnp.float32)
            total = came if total is None else total + came
        return total

    def behind(value, *boxes):
        if not boxes:
            return value
        value, *contents = lax.optimization_barrier((value, *[b[0] for b in boxes]))
        for box, content in zip(boxes, contents):
            box[0] = content
        return value

    def send(blocks, *boxes):
        blocks = [behind(b, *boxes) for b in blocks] if boxes else blocks
        return [lax.ppermute(b, "tensor", pairs[hop]) for b, hop in zip(blocks, (1, -1))]

    def to_other_core(blocks, *boxes):
        return [lax.ppermute(behind(b, *boxes) if boxes else b, "tensor", swap) for b in blocks]

    def with_other(mine, theirs):
        return [(b, 0, 1) for b in mine + theirs]


    features = own.shape[0]
    first = send([own, own])
    early = start_to_half(anchor, weights)[1]
    early16 = [early.astype(jnp.float16)]
    early_others = [other_groups_sum(early16[0])]
    grad = sort_tokens(behind(mine, [first[0]]), chips)
    came = [with_other([own], to_other_core([own])), with_other(first, to_other_core(first))]
    newest = first
    for step in range(2, half - 1):
        newest = send(newest)
        came.append(with_other(newest, to_other_core(newest)))
    head = sum(came[:2], [])
    newest = send(newest, early_others)
    sums = [gradient_part(0, features, 0, grad, head)]
    middle = sum(came[2:], [])
    sums2 = [gradient_part(0, features, len(head), grad, middle, (sums[0],))]
    skip = len(head) + len(middle)
    top = cuts[1]
    final = send([newest[0][:top], newest[1][top:]], sums)
    third = [[b] for b in newest]
    theirs = to_other_core(newest)
    theirs_final = to_other_core(final, sums2)
    tail = with_other(newest, theirs) + [(final[0], 0, 0), (final[1], top, 1), (theirs_final[0], 0, 0), (theirs_final[1], top, 1)]
    so_far = (sums2[0],)
    outs = ()
    rest = []
    for low, high in spans:
        tied = [behind(b[0], *rest) for b in tail]
        tail = [(t, *b[1:]) for t, b in zip(tied, tail)]
        gradient = gradient_part(low, high, skip, grad, tail, so_far)
        here = lambda x: x[:, low:high]
        late = late_part(gradient, *map(here, (one, two, weights, anchor)))
        late_others = other_groups_sum(late)
        rest = [[late]] if True else []
        mean = ((here(early) + here(early_others[0])) + (late.astype(jnp.float32) + late_others)) / groups
        moved = NESTEROV * here(momentum) + mean
        weight = here(anchor) - OUTER_RATE * (mean + NESTEROV * moved)
        outs = place(low, cuts[-1], (weight.astype(jnp.bfloat16), moved), outs)
    rebuilt, new_momentum = outs
    return rebuilt.T, new_momentum.T


def solution(mesh):
    placed = (
        P(("replica", "tensor"), None),
        P("replica", "tensor"),
        P("replica", "tensor"),
        P("replica", "tensor"),
        P("replica", "tensor"),
        P(None, "tensor"),
        P(None, "tensor"),
    )
    return jax.shard_map(
        on_device,
        mesh=mesh,
        in_specs=placed,
        out_specs=(P(None, "tensor"), P(None, "tensor")),
        check_vma=False,
    )
```

```python
import functools

import jax
import jax.numpy as jnp
from jax import lax
from jax.experimental import pallas as pl
from jax.experimental.pallas import tpu as pltpu
from jax.sharding import PartitionSpec as P

BETA_ONE = 0.9
BETA_TWO = 0.95
BIAS_ONE = 0.9999734386
BIAS_TWO = 0.9940794708
EPSILON = 1e-08
INNER_RATE = 0.25
DECAY_RATE = 0.1
OUTER_RATE = 0.7
NESTEROV = 0.9
CORES = 2
LANES = 128


def chip_ring(chips):
    return list(range(0, chips, 2)) + list(range(chips - 1, 0, -2))


def arrivals(chips):
    return [[0]] + [[-hop, hop] for hop in range(1, chips // 2)] + [[chips // 2]]


def ring_step(size, hop):
    ring = chip_ring(size // CORES)
    return [
        (chip * CORES + core, ring[(at + hop) % len(ring)] * CORES + core)
        for at, chip in enumerate(ring)
        for core in range(CORES)
    ]


def feature_cuts(features):
    tiles = features // LANES
    return [0, tiles // 3 * LANES, 2 * (tiles // 3) * LANES, features]

def in_vmem(limit):
    return pltpu.CompilerParams(vmem_limit_bytes=limit)


def sort_kernel(chips, grad_ref, sorted_ref, sems):
    index = lax.axis_index("tensor")
    at, core = index // CORES, index % CORES
    tokens = sorted_ref.shape[1] // (CORES * chips)
    ring = chip_ring(chips)
    place = sum(jnp.where(at == chip, spot, 0) for spot, chip in enumerate(ring))
    copies = []
    for hops in arrivals(chips):
        for side in range(CORES):
            for hop in hops:
                there = lax.rem(place + hop + chips, chips)
                chip = sum(jnp.where(there == s, c, 0) for s, c in enumerate(ring))
                block = chip * CORES + (core if side == 0 else 1 - core)
                copy = pltpu.make_async_copy(
                    grad_ref.at[:, pl.ds(pl.multiple_of(block * tokens, LANES), tokens)],
                    sorted_ref.at[:, pl.ds(len(copies) * tokens, tokens)],
                    sems.at[len(copies)],
                )
                copy.start()
                copies.append(copy)
    for copy in copies:
        copy.wait()


def sort_tokens(grad, chips):
    return pl.pallas_call(
        functools.partial(sort_kernel, chips),
        out_shape=pltpu.VMEM(grad.shape, grad.dtype),
        in_specs=[pl.BlockSpec(memory_space=pl.ANY)],
        out_specs=pl.BlockSpec(memory_space=pltpu.VMEM),
        scratch_shapes=[pltpu.SemaphoreType.DMA((CORES * chips,))],
        compiler_params=in_vmem(2**20),
        cost_estimate=pl.CostEstimate(flops=0, bytes_accessed=4 * grad.size, transcendentals=0),
        name="sort_tokens",
    )(grad)


def place_kernel(low, *refs):
    parts, outs, sems = refs[:2], refs[-3:-1], refs[-1]
    copies = [
        pltpu.make_async_copy(part, out.at[:, pl.ds(low, part.shape[1])], sems.at[at])
        for at, (part, out) in enumerate(zip(parts, outs))
    ]
    for copy in copies:
        copy.start()
    for copy in copies:
        copy.wait()


def place(low, width, parts, outs):
    return pl.pallas_call(
        functools.partial(place_kernel, low),
        out_shape=tuple(jax.ShapeDtypeStruct((p.shape[0], width), p.dtype) for p in parts),
        in_specs=[pl.BlockSpec(memory_space=pl.ANY)] * (2 + len(outs)),
        out_specs=(pl.BlockSpec(memory_space=pl.ANY),) * 2,
        scratch_shapes=[pltpu.SemaphoreType.DMA((2,))],
        input_output_aliases={2 + at: at for at in range(len(outs))},
        compiler_params=in_vmem(2**20),
        cost_estimate=pl.CostEstimate(
            flops=0, bytes_accessed=12 * parts[0].size, transcendentals=0
        ),
        name="place",
    )(*parts, *outs)


def gradient_kernel(low, skip, tops, grad_ref, *refs):
    count = len(tops)
    blocks, so_far, (out_ref, acts, sems) = refs[:count], refs[count:-3], refs[-3:]
    tokens, high = blocks[0].shape[1], low + out_ref.shape[1]
    at, copies = 0, []
    for block, (top, ends) in zip(blocks, tops):
        first, after = max(low, top), min(high, top + block.shape[0])
        if first < after:
            copy = pltpu.make_async_copy(
                block.at[pl.ds(first - top, after - first)],
                acts.at[pl.ds(first - low, after - first), pl.ds(at * tokens, tokens)],
                sems.at[len(copies)],
            )
            copy.start()
            copies.append(copy)
        at += ends
    for copy in copies:
        copy.wait()
    product = lax.dot_general(
        grad_ref[:, skip * tokens : (skip + at) * tokens],
        acts[...],
        (((1,), (1,)), ((), ())),
        preferred_element_type=jnp.float32,
    )
    for ref in so_far:
        product = ref[:, low:high] + product
    out_ref[...] = product


def gradient_part(low, high, skip, grad, blocks, so_far=()):
    rows, tokens = grad.shape[0], blocks[0][0].shape[1]
    arrays = [b[0] for b in blocks]
    depth = tokens * sum(b[2] for b in blocks)
    return pl.pallas_call(
        functools.partial(gradient_kernel, low, skip, [b[1:] for b in blocks]),
        out_shape=jax.ShapeDtypeStruct((rows, high - low), jnp.float32),
        in_specs=[pl.BlockSpec(memory_space=pltpu.VMEM)]
        + [pl.BlockSpec(memory_space=pl.ANY)] * len(arrays)
        + [pl.BlockSpec(memory_space=pltpu.VMEM)] * len(so_far),
        out_specs=pl.BlockSpec(memory_space=pltpu.VMEM),
        scratch_shapes=[
            pltpu.VMEM((high - low, depth), arrays[0].dtype),
            pltpu.SemaphoreType.DMA((len(arrays),)),
        ],
        compiler_params=in_vmem(16 * 2**20),
        cost_estimate=pl.CostEstimate(
            flops=2 * rows * (high - low) * depth, bytes_accessed=8 * rows * (high - low), transcendentals=0
        ),
        name="gradient",
    )(grad, *arrays, *so_far)


def start_to_half(anchor, weights):
    exact = anchor - (1.0 - INNER_RATE * DECAY_RATE) * weights
    return exact, lax.reduce_precision(exact, 5, 10)


def late_part(gradient, first_moment, second_moment, weights, anchor):
    moment_one = BETA_ONE * first_moment + (1.0 - BETA_ONE) * gradient
    moment_two = BETA_TWO * second_moment + (1.0 - BETA_TWO) * gradient * gradient
    step = moment_one / BIAS_ONE / (jnp.sqrt(moment_two / BIAS_TWO) + EPSILON)
    exact, half = start_to_half(anchor, weights)
    return ((exact - half) + INNER_RATE * step).astype(jnp.float16)


def on_device(
    activations, out_grad, master_weights, first_moment, second_moment, anchor, outer_momentum
):
    size = lax.axis_size("tensor")
    groups = lax.axis_size("replica")
    chips = size // CORES
    half = chips // 2
    pairs = {hop: ring_step(size, hop) for hop in (1, -1)}
    swap = [(d, d ^ 1) for d in range(size)]
    own, mine = activations.T, out_grad.T
    weights, one, two = master_weights.T, first_moment.T, second_moment.T
    anchor, momentum = anchor.T, outer_momentum.T
    cuts = feature_cuts(own.shape[0])
    spans = list(zip(cuts[:-1], cuts[1:]))

    def other_groups_sum(value):
        total = None
        for hop in range(1, groups):
            there = [(g, (g + hop) % groups) for g in range(groups)]
            came = lax.ppermute(value, "replica", there).astype(jnp.float32)
            total = came if total is None else total + came
        return total

    def behind(value, *boxes):
        if not boxes:
            return value
        value, *contents = lax.optimization_barrier((value, *[b[0] for b in boxes]))
        for box, content in zip(boxes, contents):
            box[0] = content
        return value

    def send(blocks, *boxes):
        blocks = [behind(b, *boxes) for b in blocks] if boxes else blocks
        return [lax.ppermute(b, "tensor", pairs[hop]) for b, hop in zip(blocks, (1, -1))]

    def to_other_core(blocks, *boxes):
        return [lax.ppermute(behind(b, *boxes) if boxes else b, "tensor", swap) for b in blocks]

    def with_other(mine, theirs):
        return [(b, 0, 1) for b in mine + theirs]


    features = own.shape[0]
    first = send([own, own])
    early = start_to_half(anchor, weights)[1]
    early16 = [early.astype(jnp.float16)]
    early_others = [other_groups_sum(early16[0])]
    grad = sort_tokens(behind(mine, [first[0]]), chips)
    came = [with_other([own], to_other_core([own])), with_other(first, to_other_core(first))]
    head = sum(came, [])
    sums = [gradient_part(0, features, 0, grad, head)]
    newest = first
    middle = []
    for step in range(2, half - 1):
        newest = send(newest)
        middle += with_other(newest, to_other_core(newest))
    newest = send(newest)
    top = features // 2
    final = send([newest[0][:top], newest[1][top:]], *[early_others, sums])
    theirs = to_other_core(newest)
    sums2 = [gradient_part(0, features, len(head), grad, middle, (sums[0],))]
    skip = len(head) + len(middle)
    theirs_final = to_other_core(final, *[sums2])
    tail = with_other(newest, theirs) + [(final[0], 0, 0), (final[1], top, 1), (theirs_final[0], 0, 0), (theirs_final[1], top, 1)]
    so_far = (sums2[0],)
    outs = ()
    rest = []
    for low, high in spans:
        tied = [behind(b[0], *rest) for b in tail]
        tail = [(t, *b[1:]) for t, b in zip(tied, tail)]
        gradient = gradient_part(low, high, skip, grad, tail, so_far)
        here = lambda x: x[:, low:high]
        late = late_part(gradient, *map(here, (one, two, weights, anchor)))
        late_others = other_groups_sum(late)
        rest = [[late]] if True else []
        mean = ((here(early) + here(early_others[0])) + (late.astype(jnp.float32) + late_others)) / groups
        moved = NESTEROV * here(momentum) + mean
        weight = here(anchor) - OUTER_RATE * (mean + NESTEROV * moved)
        outs = place(low, cuts[-1], (weight.astype(jnp.bfloat16), moved), outs)
    rebuilt, new_momentum = outs
    return rebuilt.T, new_momentum.T


def solution(mesh):
    placed = (
        P(("replica", "tensor"), None),
        P("replica", "tensor"),
        P("replica", "tensor"),
        P("replica", "tensor"),
        P("replica", "tensor"),
        P(None, "tensor"),
        P(None, "tensor"),
    )
    return jax.shard_map(
        on_device,
        mesh=mesh,
        in_specs=placed,
        out_specs=(P(None, "tensor"), P(None, "tensor")),
        check_vma=False,
    )
```

```python
import functools

import jax
import jax.numpy as jnp
from jax import lax
from jax.experimental import pallas as pl
from jax.experimental.pallas import tpu as pltpu
from jax.sharding import PartitionSpec as P

BETA_ONE = 0.9
BETA_TWO = 0.95
BIAS_ONE = 0.9999734386
BIAS_TWO = 0.9940794708
EPSILON = 1e-08
INNER_RATE = 0.25
DECAY_RATE = 0.1
OUTER_RATE = 0.7
NESTEROV = 0.9
CORES = 2
LANES = 128


def chip_ring(chips):
    return list(range(0, chips, 2)) + list(range(chips - 1, 0, -2))


def arrivals(chips):
    return [[0]] + [[-hop, hop] for hop in range(1, chips // 2)] + [[chips // 2]]


def ring_step(size, hop):
    ring = chip_ring(size // CORES)
    return [
        (chip * CORES + core, ring[(at + hop) % len(ring)] * CORES + core)
        for at, chip in enumerate(ring)
        for core in range(CORES)
    ]


def feature_cuts(features):
    tiles = features // LANES
    return [0, tiles // 3 * LANES, (tiles - 1) * LANES, features]


def in_vmem(limit):
    return pltpu.CompilerParams(vmem_limit_bytes=limit)


def sort_kernel(chips, grad_ref, sorted_ref, sems):
    index = lax.axis_index("tensor")
    at, core = index // CORES, index % CORES
    tokens = sorted_ref.shape[1] // (CORES * chips)
    ring = chip_ring(chips)
    place = sum(jnp.where(at == chip, spot, 0) for spot, chip in enumerate(ring))
    copies = []
    for hops in arrivals(chips):
        for side in range(CORES):
            for hop in hops:
                there = lax.rem(place + hop + chips, chips)
                chip = sum(jnp.where(there == s, c, 0) for s, c in enumerate(ring))
                block = chip * CORES + (core if side == 0 else 1 - core)
                copy = pltpu.make_async_copy(
                    grad_ref.at[:, pl.ds(pl.multiple_of(block * tokens, LANES), tokens)],
                    sorted_ref.at[:, pl.ds(len(copies) * tokens, tokens)],
                    sems.at[len(copies)],
                )
                copy.start()
                copies.append(copy)
    for copy in copies:
        copy.wait()


def sort_tokens(grad, chips):
    return pl.pallas_call(
        functools.partial(sort_kernel, chips),
        out_shape=pltpu.VMEM(grad.shape, grad.dtype),
        in_specs=[pl.BlockSpec(memory_space=pl.ANY)],
        out_specs=pl.BlockSpec(memory_space=pltpu.VMEM),
        scratch_shapes=[pltpu.SemaphoreType.DMA((CORES * chips,))],
        compiler_params=in_vmem(2**20),
        cost_estimate=pl.CostEstimate(flops=0, bytes_accessed=4 * grad.size, transcendentals=0),
        name="sort_tokens",
    )(grad)


def place_kernel(low, *refs):
    parts, outs, sems = refs[:2], refs[-3:-1], refs[-1]
    copies = [
        pltpu.make_async_copy(part, out.at[:, pl.ds(low, part.shape[1])], sems.at[at])
        for at, (part, out) in enumerate(zip(parts, outs))
    ]
    for copy in copies:
        copy.start()
    for copy in copies:
        copy.wait()


def place(low, width, parts, outs):
    return pl.pallas_call(
        functools.partial(place_kernel, low),
        out_shape=tuple(jax.ShapeDtypeStruct((p.shape[0], width), p.dtype) for p in parts),
        in_specs=[pl.BlockSpec(memory_space=pl.ANY)] * (2 + len(outs)),
        out_specs=(pl.BlockSpec(memory_space=pl.ANY),) * 2,
        scratch_shapes=[pltpu.SemaphoreType.DMA((2,))],
        input_output_aliases={2 + at: at for at in range(len(outs))},
        compiler_params=in_vmem(2**20),
        cost_estimate=pl.CostEstimate(
            flops=0, bytes_accessed=12 * parts[0].size, transcendentals=0
        ),
        name="place",
    )(*parts, *outs)


def gradient_kernel(low, skip, tops, grad_ref, *refs):
    count = len(tops)
    blocks, so_far, (out_ref, acts, sems) = refs[:count], refs[count:-3], refs[-3:]
    tokens, high = blocks[0].shape[1], low + out_ref.shape[1]
    at, copies = 0, []
    for block, (top, ends) in zip(blocks, tops):
        first, after = max(low, top), min(high, top + block.shape[0])
        if first < after:
            copy = pltpu.make_async_copy(
                block.at[pl.ds(first - top, after - first)],
                acts.at[pl.ds(first - low, after - first), pl.ds(at * tokens, tokens)],
                sems.at[len(copies)],
            )
            copy.start()
            copies.append(copy)
        at += ends
    for copy in copies:
        copy.wait()
    product = lax.dot_general(
        grad_ref[:, skip * tokens : (skip + at) * tokens],
        acts[...],
        (((1,), (1,)), ((), ())),
        preferred_element_type=jnp.float32,
    )
    for ref in so_far:
        product = ref[:, low:high] + product
    out_ref[...] = product


def gradient_part(low, high, skip, grad, blocks, so_far=()):
    rows, tokens = grad.shape[0], blocks[0][0].shape[1]
    arrays = [b[0] for b in blocks]
    depth = tokens * sum(b[2] for b in blocks)
    return pl.pallas_call(
        functools.partial(gradient_kernel, low, skip, [b[1:] for b in blocks]),
        out_shape=jax.ShapeDtypeStruct((rows, high - low), jnp.float32),
        in_specs=[pl.BlockSpec(memory_space=pltpu.VMEM)]
        + [pl.BlockSpec(memory_space=pl.ANY)] * len(arrays)
        + [pl.BlockSpec(memory_space=pltpu.VMEM)] * len(so_far),
        out_specs=pl.BlockSpec(memory_space=pltpu.VMEM),
        scratch_shapes=[
            pltpu.VMEM((high - low, depth), arrays[0].dtype),
            pltpu.SemaphoreType.DMA((len(arrays),)),
        ],
        compiler_params=in_vmem(16 * 2**20),
        cost_estimate=pl.CostEstimate(
            flops=2 * rows * (high - low) * depth, bytes_accessed=8 * rows * (high - low), transcendentals=0
        ),
        name="gradient",
    )(grad, *arrays, *so_far)


def start_to_half(anchor, weights):
    exact = anchor - (1.0 - INNER_RATE * DECAY_RATE) * weights
    return exact, lax.reduce_precision(exact, 5, 10)


def late_part(gradient, first_moment, second_moment, weights, anchor):
    moment_one = BETA_ONE * first_moment + (1.0 - BETA_ONE) * gradient
    moment_two = BETA_TWO * second_moment + (1.0 - BETA_TWO) * gradient * gradient
    step = moment_one / BIAS_ONE / (jnp.sqrt(moment_two / BIAS_TWO) + EPSILON)
    exact, half = start_to_half(anchor, weights)
    return ((exact - half) + INNER_RATE * step).astype(jnp.float16)


def on_device(
    activations, out_grad, master_weights, first_moment, second_moment, anchor, outer_momentum
):
    size = lax.axis_size("tensor")
    groups = lax.axis_size("replica")
    chips = size // CORES
    half = chips // 2
    pairs = {hop: ring_step(size, hop) for hop in (1, -1)}
    swap = [(d, d ^ 1) for d in range(size)]
    own, mine = activations.T, out_grad.T
    weights, one, two = master_weights.T, first_moment.T, second_moment.T
    anchor, momentum = anchor.T, outer_momentum.T
    features = own.shape[0]
    cuts = feature_cuts(features)
    spans = list(zip(cuts[:-1], cuts[1:]))

    def across(value):
        if groups != 2:
            return lax.psum(value.astype(jnp.float32), "replica")
        return lax.ppermute(value, "replica", [(0, 1), (1, 0)]).astype(jnp.float32)

    def total(value, came):
        return value + came if groups == 2 else came

    def across_packed(value):
        rows, count = value.shape
        spare = count % LANES
        if groups != 2 or 2 * spare != LANES or rows % 32:
            return across(value)
        tiles = [value[:, at : at + LANES] for at in range(0, count - spare, LANES)]
        rest = value[:, count - spare :]
        tiles.append(jnp.concatenate([rest[: rows // 2], rest[rows // 2 :]], axis=1))
        other = across(jnp.concatenate(tiles))
        parts = [other[at * rows : (at + 1) * rows] for at in range(len(tiles) - 1)]
        rest = other[(len(tiles) - 1) * rows :]
        parts.append(jnp.concatenate([rest[:, :spare], rest[:, spare:]]))
        return jnp.concatenate(parts, axis=1)

    def behind(value, *boxes):
        if not boxes:
            return value
        value, *contents = lax.optimization_barrier((value, *[b[0] for b in boxes]))
        for box, content in zip(boxes, contents):
            box[0] = content
        return value

    def send(blocks, *boxes):
        blocks = [behind(b, *boxes) for b in blocks]
        return [lax.ppermute(b, "tensor", pairs[hop]) for b, hop in zip(blocks, (1, -1))]

    def with_other_core(blocks, *boxes):
        return blocks + [lax.ppermute(behind(b, *boxes), "tensor", swap) for b in blocks]

    def whole(blocks):
        return [(b, 0, 1) for b in blocks]

    first = send([own, own])
    early = start_to_half(anchor, weights)[1]
    early_came = [across(early.astype(jnp.float16))]
    grad = sort_tokens(behind(mine, [first[0]]), chips)
    head = whole(with_other_core([own]) + with_other_core(first))
    head_sum = [gradient_part(0, features, 0, grad, head)]
    newest, middle = first, []
    for step in range(2, half - 1):
        newest = send(newest)
        middle += whole(with_other_core(newest))
    newest = send(newest)
    top = features // 2
    opposite = send([newest[0][:top], newest[1][top:]], early_came, head_sum)
    third = whole(with_other_core(newest))
    so_far = [gradient_part(0, features, len(head), grad, middle, (head_sum[0],))]
    skip = len(head) + len(middle)
    ends = [(0, 0), (top, 1)] * CORES
    tail = third + [(b, *end) for b, end in zip(with_other_core(opposite, so_far), ends)]

    lates, came, outs = [], [], ()
    for low, high in spans:
        ties = lates[-1:] + came[-2:-1]
        tail = [(behind(b[0], *ties), *b[1:]) for b in tail]
        gradient = gradient_part(low, high, skip, grad, tail, (so_far[0],))
        late = late_part(gradient, *[x[:, low:high] for x in (one, two, weights, anchor)])
        lates.append([late])
        came.append([across_packed(late)])
    for (low, high), (late,), (other,) in zip(spans, lates, came):
        here = lambda x: x[:, low:high]
        mean = (total(here(early), here(early_came[0])) + total(late.astype(jnp.float32), other)) / groups
        moved = NESTEROV * here(momentum) + mean
        weight = here(anchor) - OUTER_RATE * (mean + NESTEROV * moved)
        outs = place(low, features, (weight.astype(jnp.bfloat16), moved), outs)
    rebuilt, new_momentum = outs
    return rebuilt.T, new_momentum.T


def solution(mesh):
    placed = (
        P(("replica", "tensor"), None),
        P("replica", "tensor"),
        P("replica", "tensor"),
        P("replica", "tensor"),
        P("replica", "tensor"),
        P(None, "tensor"),
        P(None, "tensor"),
    )
    return jax.shard_map(
        on_device,
        mesh=mesh,
        in_specs=placed,
        out_specs=(P(None, "tensor"), P(None, "tensor")),
        check_vma=False,
    )
```

```python
import functools

import jax
import jax.numpy as jnp
from jax import lax
from jax.experimental import pallas as pl
from jax.experimental.pallas import tpu as pltpu
from jax.sharding import PartitionSpec as P

BETA_ONE = 0.9
BETA_TWO = 0.95
BIAS_ONE = 0.9999734386
BIAS_TWO = 0.9940794708
EPSILON = 1e-08
INNER_RATE = 0.25
DECAY_RATE = 0.1
OUTER_RATE = 0.7
NESTEROV = 0.9
CORES = 2
LANES = 128


def chip_ring(chips):
    return list(range(0, chips, 2)) + list(range(chips - 1, 0, -2))


def arrivals(chips):
    return [[0]] + [[-hop, hop] for hop in range(1, chips // 2)] + [[chips // 2]]


def ring_step(size, hop):
    ring = chip_ring(size // CORES)
    return [
        (chip * CORES + core, ring[(at + hop) % len(ring)] * CORES + core)
        for at, chip in enumerate(ring)
        for core in range(CORES)
    ]


def feature_cuts(features):
    tiles = features // LANES
    return [0, tiles // 3 * LANES, (tiles - 1) * LANES, features]


def in_vmem(limit):
    return pltpu.CompilerParams(vmem_limit_bytes=limit)


def sort_kernel(chips, grad_ref, sorted_ref, sems):
    index = lax.axis_index("tensor")
    at, core = index // CORES, index % CORES
    tokens = sorted_ref.shape[1] // (CORES * chips)
    ring = chip_ring(chips)
    place = sum(jnp.where(at == chip, spot, 0) for spot, chip in enumerate(ring))
    copies = []
    for hops in arrivals(chips):
        for side in range(CORES):
            for hop in hops:
                there = lax.rem(place + hop + chips, chips)
                chip = sum(jnp.where(there == s, c, 0) for s, c in enumerate(ring))
                block = chip * CORES + (core if side == 0 else 1 - core)
                copy = pltpu.make_async_copy(
                    grad_ref.at[:, pl.ds(pl.multiple_of(block * tokens, LANES), tokens)],
                    sorted_ref.at[:, pl.ds(len(copies) * tokens, tokens)],
                    sems.at[len(copies)],
                )
                copy.start()
                copies.append(copy)
    for copy in copies:
        copy.wait()


def sort_tokens(grad, chips):
    return pl.pallas_call(
        functools.partial(sort_kernel, chips),
        out_shape=pltpu.VMEM(grad.shape, grad.dtype),
        in_specs=[pl.BlockSpec(memory_space=pl.ANY)],
        out_specs=pl.BlockSpec(memory_space=pltpu.VMEM),
        scratch_shapes=[pltpu.SemaphoreType.DMA((CORES * chips,))],
        compiler_params=in_vmem(2**20),
        cost_estimate=pl.CostEstimate(flops=0, bytes_accessed=4 * grad.size, transcendentals=0),
        name="sort_tokens",
    )(grad)


def place_kernel(low, *refs):
    parts, outs, sems = refs[:2], refs[-3:-1], refs[-1]
    copies = [
        pltpu.make_async_copy(part, out.at[:, pl.ds(low, part.shape[1])], sems.at[at])
        for at, (part, out) in enumerate(zip(parts, outs))
    ]
    for copy in copies:
        copy.start()
    for copy in copies:
        copy.wait()


def place(low, width, parts, outs):
    return pl.pallas_call(
        functools.partial(place_kernel, low),
        out_shape=tuple(jax.ShapeDtypeStruct((p.shape[0], width), p.dtype) for p in parts),
        in_specs=[pl.BlockSpec(memory_space=pl.ANY)] * (2 + len(outs)),
        out_specs=(pl.BlockSpec(memory_space=pl.ANY),) * 2,
        scratch_shapes=[pltpu.SemaphoreType.DMA((2,))],
        input_output_aliases={2 + at: at for at in range(len(outs))},
        compiler_params=in_vmem(2**20),
        cost_estimate=pl.CostEstimate(
            flops=0, bytes_accessed=12 * parts[0].size, transcendentals=0
        ),
        name="place",
    )(*parts, *outs)


def gradient_kernel(low, skip, tops, grad_ref, *refs):
    count = len(tops)
    blocks, so_far, (out_ref, acts, sems) = refs[:count], refs[count:-3], refs[-3:]
    tokens, high = blocks[0].shape[1], low + out_ref.shape[1]
    at, copies = 0, []
    for block, (top, ends) in zip(blocks, tops):
        first, after = max(low, top), min(high, top + block.shape[0])
        if first < after:
            copy = pltpu.make_async_copy(
                block.at[pl.ds(first - top, after - first)],
                acts.at[pl.ds(first - low, after - first), pl.ds(at * tokens, tokens)],
                sems.at[len(copies)],
            )
            copy.start()
            copies.append(copy)
        at += ends
    for copy in copies:
        copy.wait()
    product = lax.dot_general(
        grad_ref[:, skip * tokens : (skip + at) * tokens],
        acts[...],
        (((1,), (1,)), ((), ())),
        preferred_element_type=jnp.float32,
    )
    for ref in so_far:
        product = ref[:, low:high] + product
    out_ref[...] = product


def gradient_part(low, high, skip, grad, blocks, so_far=()):
    rows, tokens = grad.shape[0], blocks[0][0].shape[1]
    arrays = [b[0] for b in blocks]
    depth = tokens * sum(b[2] for b in blocks)
    return pl.pallas_call(
        functools.partial(gradient_kernel, low, skip, [b[1:] for b in blocks]),
        out_shape=jax.ShapeDtypeStruct((rows, high - low), jnp.float32),
        in_specs=[pl.BlockSpec(memory_space=pltpu.VMEM)]
        + [pl.BlockSpec(memory_space=pl.ANY)] * len(arrays)
        + [pl.BlockSpec(memory_space=pltpu.VMEM)] * len(so_far),
        out_specs=pl.BlockSpec(memory_space=pltpu.VMEM),
        scratch_shapes=[
            pltpu.VMEM((high - low, depth), arrays[0].dtype),
            pltpu.SemaphoreType.DMA((len(arrays),)),
        ],
        compiler_params=in_vmem(16 * 2**20),
        cost_estimate=pl.CostEstimate(
            flops=2 * rows * (high - low) * depth, bytes_accessed=8 * rows * (high - low), transcendentals=0
        ),
        name="gradient",
    )(grad, *arrays, *so_far)


def start_to_half(anchor, weights):
    exact = anchor - (1.0 - INNER_RATE * DECAY_RATE) * weights
    return exact, lax.reduce_precision(exact, 5, 10)


def late_part(gradient, first_moment, second_moment, weights, anchor):
    moment_one = BETA_ONE * first_moment + (1.0 - BETA_ONE) * gradient
    moment_two = BETA_TWO * second_moment + (1.0 - BETA_TWO) * gradient * gradient
    step = moment_one / BIAS_ONE / (jnp.sqrt(moment_two / BIAS_TWO) + EPSILON)
    exact, half = start_to_half(anchor, weights)
    return ((exact - half) + INNER_RATE * step).astype(jnp.float16)


def on_device(
    activations, out_grad, master_weights, first_moment, second_moment, anchor, outer_momentum
):
    size = lax.axis_size("tensor")
    groups = lax.axis_size("replica")
    chips = size // CORES
    half = chips // 2
    pairs = {hop: ring_step(size, hop) for hop in (1, -1)}
    swap = [(d, d ^ 1) for d in range(size)]
    own, mine = activations.T, out_grad.T
    weights, one, two = master_weights.T, first_moment.T, second_moment.T
    anchor, momentum = anchor.T, outer_momentum.T
    features = own.shape[0]
    cuts = feature_cuts(features)
    spans = list(zip(cuts[:-1], cuts[1:]))

    def across(value):
        if groups != 2:
            return lax.psum(value.astype(jnp.float32), "replica")
        return lax.ppermute(value, "replica", [(0, 1), (1, 0)]).astype(jnp.float32)

    def total(value, came):
        return value + came if groups == 2 else came

    def across_packed(value):
        rows, count = value.shape
        spare = count % LANES
        if groups != 2 or 2 * spare != LANES or rows % 32:
            return across(value)
        tiles = [value[:, at : at + LANES] for at in range(0, count - spare, LANES)]
        rest = value[:, count - spare :]
        tiles.append(jnp.concatenate([rest[: rows // 2], rest[rows // 2 :]], axis=1))
        other = across(jnp.concatenate(tiles))
        parts = [other[at * rows : (at + 1) * rows] for at in range(len(tiles) - 1)]
        rest = other[(len(tiles) - 1) * rows :]
        parts.append(jnp.concatenate([rest[:, :spare], rest[:, spare:]]))
        return jnp.concatenate(parts, axis=1)

    def behind(value, *boxes):
        if not boxes:
            return value
        value, *contents = lax.optimization_barrier((value, *[b[0] for b in boxes]))
        for box, content in zip(boxes, contents):
            box[0] = content
        return value

    def send(blocks, *boxes):
        blocks = [behind(b, *boxes) for b in blocks]
        return [lax.ppermute(b, "tensor", pairs[hop]) for b, hop in zip(blocks, (1, -1))]

    def with_other_core(blocks, *boxes):
        return blocks + [lax.ppermute(behind(b, *boxes), "tensor", swap) for b in blocks]

    def whole(blocks):
        return [(b, 0, 1) for b in blocks]

    first = send([own, own])
    early = start_to_half(anchor, weights)[1]
    early_came = [across(early.astype(jnp.float16))]
    grad = sort_tokens(mine, chips)
    head = whole(with_other_core([own]) + with_other_core(first))
    head_sum = [gradient_part(0, features, 0, grad, head)]
    newest, middle = first, []
    for step in range(2, half - 1):
        newest = send(newest)
        middle += whole(with_other_core(newest))
    newest = send(newest)
    top = features // 2
    opposite = send([newest[0][:top], newest[1][top:]], early_came, head_sum)
    third = whole(with_other_core(newest))
    so_far = [gradient_part(0, features, len(head), grad, middle, (head_sum[0],))]
    skip = len(head) + len(middle)
    ends = [(0, 0), (top, 1)] * CORES
    tail = third + [(b, *end) for b, end in zip(with_other_core(opposite, so_far), ends)]

    lates, came, outs = [], [], ()
    for low, high in spans:
        ties = lates[-1:] + came[-2:-1]
        tail = [(behind(b[0], *ties), *b[1:]) for b in tail]
        gradient = gradient_part(low, high, skip, grad, tail, (so_far[0],))
        late = late_part(gradient, *[x[:, low:high] for x in (one, two, weights, anchor)])
        lates.append([late])
        came.append([across_packed(late)])
    for (low, high), (late,), (other,) in zip(spans, lates, came):
        here = lambda x: x[:, low:high]
        mean = (total(here(early), here(early_came[0])) + total(late.astype(jnp.float32), other)) / groups
        moved = NESTEROV * here(momentum) + mean
        weight = here(anchor) - OUTER_RATE * (mean + NESTEROV * moved)
        outs = place(low, features, (weight.astype(jnp.bfloat16), moved), outs)
    rebuilt, new_momentum = outs
    return rebuilt.T, new_momentum.T


def solution(mesh):
    placed = (
        P(("replica", "tensor"), None),
        P("replica", "tensor"),
        P("replica", "tensor"),
        P("replica", "tensor"),
        P("replica", "tensor"),
        P(None, "tensor"),
        P(None, "tensor"),
    )
    return jax.shard_map(
        on_device,
        mesh=mesh,
        in_specs=placed,
        out_specs=(P(None, "tensor"), P(None, "tensor")),
        check_vma=False,
    )
```
